32 devices in a mesh: imp: 8 (over z, x), adv: 4 (over y, core).
Axes of the slice: x: 2, y: 2, z: 4, core: 2. Of those that a mesh axis runs over, the one named last changes fastest.
Arguments:
- impression_vectors: bfloat16 [64, 16384], P(None, 'imp'), may hold values from -6 to 6
- advertiser_vectors: bfloat16 [64, 4096], P(None, ('imp', 'adv')), may hold values from -0.75 to 0.75
- spend_limits: float32 [4096], P(('imp', 'adv')), may hold values from 1024 to 8192
- capacity: float32 [16384], P('imp'), may hold values from 256 to 2048
- blocks: int32 [128, 4, 8], P('imp', 'adv'), may hold values from 0 to 31, as said below
- counts: int32 [128, 4], P('imp', 'adv'), may hold values from 1 to 8, as said below
Outputs:
- prices: float32 [4096], P(('imp', 'adv'))
- impression_duals: float32 [16384], P('imp')
- impression_grad: bfloat16 [64, 16384], P(None, ('imp', 'adv'))
- advertiser_grad: bfloat16 [64, 4096], P(None, ('imp', 'adv'))
The draws below stay inside these ranges and needn't reach their ends.
Inputs may be any that keep to these rules, and one draw needn't show every extreme that they name: Block numbers. Entry [g, a, k] names a block b with (b) % (the size of adv) == a. The 8 entries of one list are distinct; entries at slots k >= counts[g, a] are padding and name valid blocks too. `counts`: every group has one index of adv whose count is 8.
All inputs are finite; a program needn't handle non-finite values.
Results may differ from the reference program's by a relative error of at most 0.012.
Values may be sent and summed in bfloat16 or wider, within the bound.
A program may use at most 64 MiB of HBM per device.

```python
import math
import jax
import jax.numpy as jnp
from jax import lax

E = 64
GROUP = 128
BLOCK = 128
K = 8
ITERS = 3
BLK_DEV = 1
GROUPS = 128
IMPRESSIONS = 16384
ADV = 4096
N_IMP = 8
N_ADV = 4


def draw_blocks(key, part):
    served = BLK_DEV * N_IMP
    scores = jax.random.randint(key, (GROUPS, N_ADV, served), 0, 1 << 20) * served + jnp.arange(served)
    ranking = jnp.argsort(scores, axis=-1, stable=True)[..., :K]
    holder = ranking // BLK_DEV
    inside = ranking % BLK_DEV
    owning = jnp.arange(N_ADV)[None, :, None]
    return ((holder * N_ADV + owning) * BLK_DEV + inside).astype(jnp.int32)


def draw_counts(key, part):
    first_key, second_key, third_key = jax.random.split(jax.random.fold_in(key, 7), 3)
    first = jax.random.randint(first_key, (GROUPS, N_ADV), 1, K + 1)
    second = jax.random.randint(second_key, (GROUPS, N_ADV), 1, K + 1)
    lesser = jnp.minimum(first, second)
    anchor = jax.random.randint(third_key, (GROUPS, 1), 0, N_ADV)
    return jnp.where(jnp.arange(N_ADV)[None, :] == anchor, K, lesser).astype(jnp.int32)


def block_levels(rng, shape, cuts, smallest, high):
    level, own = 1.0, jax.random.fold_in(rng, 6)
    for dim, shards_of in cuts:
        heights = jnp.exp(jax.random.uniform(jax.random.fold_in(own, dim), (shards_of,), jnp.float32, smallest / len(cuts), high / len(cuts)))
        level = level * jnp.repeat(heights, shape[dim] // shards_of).reshape([-1 if axis == dim else 1 for axis in range(len(shape))])
    return level


def scatter_about(stream_key, shape, deviation, reach, cuts=(), held_as=jnp.bfloat16):
    drawn = jax.random.normal(stream_key, shape, jnp.float32) * deviation
    if len(cuts) > 0:
        drawn = block_levels(stream_key, shape, cuts, -0.22, 0.18) * drawn
    return jnp.clip(drawn, min=-reach, max=reach).astype(held_as)


def setup_inputs(seed: int = 0) -> dict:
    splits = jax.random.split(jax.random.key(seed), 7)
    return {
        "impression_vectors": scatter_about(splits[0], (E, IMPRESSIONS), 1.0, 6.0, ((1, 8),)),
        "advertiser_vectors": scatter_about(splits[1], (E, ADV), E ** -0.5, 0.75, ((1, 32),)),
        "spend_limits": jnp.clip(jnp.exp(math.log(8192.0) - 2.0794415 * jax.random.uniform(splits[2], (ADV,), jnp.float32) ** block_levels(splits[2], (ADV,), ((0, 32),), -0.2, 0.2)), 1024.0, 8192.0),
        "capacity": jnp.clip(jnp.exp(math.log(2048.0) - 2.0794415 * jax.random.uniform(splits[3], (IMPRESSIONS,), jnp.float32) ** block_levels(splits[3], (IMPRESSIONS,), ((0, 8),), -0.2, 0.2)), 256.0, 2048.0),
        "blocks": draw_blocks(jax.random.fold_in(splits[6], 71), 0),
        "counts": draw_counts(jax.random.fold_in(splits[6], 71), 0),
    }


def reference(impression_vectors, advertiser_vectors, spend_limits, capacity, blocks, counts):
    groups = blocks.shape[0]
    features = impression_vectors.shape[0]
    block_total = advertiser_vectors.shape[1] // BLOCK
    block_ids = blocks.reshape(groups, -1)
    live_slots = (jnp.arange(K)[None, None, :] < counts[:, :, None]).reshape(groups, -1).astype(jnp.float32)
    catalog = advertiser_vectors.reshape(features, block_total, BLOCK)
    viewers = impression_vectors.reshape(features, groups, GROUP)
    extent = block_ids.shape[1] * BLOCK

    def allocate(prices, duals, group_no):
        chosen = block_ids[group_no]
        columns = jnp.take(catalog, chosen, axis=1).reshape(features, extent)
        viewer = lax.dynamic_index_in_dim(viewers, group_no, 1, keepdims=False)
        scores = jnp.dot(viewer.T, columns, preferred_element_type=jnp.float32)
        charged = jnp.take(prices.reshape(block_total, BLOCK), chosen, axis=0).reshape(extent)
        shadow = lax.dynamic_slice_in_dim(duals, group_no * GROUP, GROUP)
        eligible = jnp.repeat(live_slots[group_no], BLOCK)
        shares = jnp.clip(scores - charged[None, :] - shadow[:, None], 0.0, 1.0) * eligible[None, :]
        return shares, chosen, columns, viewer

    def totals(prices, duals):
        def advance(outlay, group_no):
            shares, chosen, _, _ = allocate(prices, duals, group_no)
            outlay = outlay.at[chosen].add(jnp.sum(shares, axis=0).reshape(-1, BLOCK))
            return outlay, jnp.sum(shares, axis=1)

        outlay, demand = lax.scan(advance, jnp.zeros((block_total, BLOCK), jnp.float32), jnp.arange(groups))
        return outlay.reshape(-1), demand.reshape(-1)

    prices = jnp.zeros((block_total * BLOCK,), jnp.float32)
    duals = jnp.zeros((groups * GROUP,), jnp.float32)
    for iteration in range(ITERS):
        outlay, demand = totals(prices, duals)
        prices = jnp.maximum(prices + outlay / spend_limits - 1.0, 0.0)
        duals = jnp.maximum(duals + demand / capacity - 1.0, 0.0)

    row_groups = groups // N_IMP

    def row_step(running, row_index):
        def group_step(partial_value, offset):
            shares, chosen, columns, viewer = allocate(prices, duals, row_index * row_groups + offset)
            weights = shares.astype(jnp.bfloat16)
            imp_cols = jnp.dot(columns, weights.T, preferred_element_type=jnp.float32)
            adv_terms = jnp.dot(viewer, weights, preferred_element_type=jnp.float32).reshape(features, -1, BLOCK)
            partial_value = partial_value.at[:, chosen].add(adv_terms)
            return partial_value, imp_cols

        partial_value, imp_cols = lax.scan(group_step, jnp.zeros((features, block_total, BLOCK), jnp.float32), jnp.arange(row_groups))
        rounded = lax.optimization_barrier((partial_value / GROUP).astype(jnp.bfloat16)).astype(jnp.float32)
        return running + rounded, imp_cols

    running, imp_cols = lax.scan(row_step, jnp.zeros((features, block_total, BLOCK), jnp.float32), jnp.arange(N_IMP))
    impression_grad = jnp.transpose(imp_cols, (2, 0, 1, 3)).reshape(features, -1).astype(jnp.bfloat16)
    advertiser_grad = running.reshape(features, -1).astype(jnp.bfloat16)
    return prices, duals, impression_grad, advertiser_grad
```

```python
import functools

import jax
import jax.numpy as jnp
from jax import lax
from jax.experimental import pallas as pl
from jax.experimental.pallas import tpu as pltpu
from jax.sharding import PartitionSpec as P

GROUP = 128
BLOCK = 128
ITERS = 3
FAR = 32768.0
ROWS = 16
MESH = pl.DeviceIdType.MESH
F32 = jnp.float32
BF16 = jnp.bfloat16


def pieces(x):
    a = x.astype(BF16).astype(F32)
    b = (x - a).astype(BF16).astype(F32)
    return a, b, x - a - b


def kernel(
    n_imp, n_adv, sizes,
    v_ref, a_ref, lim_ref, cap_ref, blk_ref, cnt_ref,
    prices_ref, duals_ref, ig_ref, ag_ref,
    vaug, aaug, at, cat, limb, lims, acc, outb, demb, pr, du, w,
    igs, igr, igown, ags, agr,
    g_send, g_recv, l_send, l_recv, o_send, o_recv, d_send, d_recv,
    i_send, i_recv, a_send, a_recv,
):
    feats, groups, slots, depth, wide, tall = sizes
    me_i, me_a = lax.axis_index("imp"), lax.axis_index("adv")
    imps = groups * GROUP
    advs = n_imp * BLOCK
    share = imps // n_adv

    def peer_i(s):
        return lax.rem(me_i + s, n_imp)

    def peer_a(s):
        return lax.rem(me_a + s, n_adv)

    def send(src, dst, ssem, rsem, device):
        return pltpu.make_async_remote_copy(
            src_ref=src, dst_ref=dst, send_sem=ssem, recv_sem=rsem, device_id=device, device_id_type=MESH
        )

    barrier = pltpu.get_barrier_semaphore()
    for s in range(1, n_imp):
        pl.semaphore_signal(barrier, inc=1, device_id={"imp": peer_i(s)}, device_id_type=MESH)
    for s in range(1, n_adv):
        pl.semaphore_signal(barrier, inc=1, device_id={"adv": peer_a(s)}, device_id_type=MESH)
    pl.semaphore_wait(barrier, n_imp + n_adv - 2)

    def gather_copies(s):
        there = {"imp": peer_i(s)}
        return (
            send(a_ref, cat.at[me_i], g_send.at[s], g_recv.at[s], there),
            send(lim_ref, limb.at[me_i], l_send.at[s], l_recv.at[s], there),
        )

    for s in range(1, n_imp):
        for copy in gather_copies(s):
            copy.start()

    head = feats
    mask_at = feats + ROWS
    cat[me_i] = a_ref[...]
    limb[me_i] = lim_ref[...]
    vaug[0:feats, :] = v_ref[...]
    vaug[mask_at:depth, :] = jnp.where(
        lax.broadcasted_iota(jnp.int32, (depth - mask_at, imps), 0)
        == lax.broadcasted_iota(jnp.int32, (depth - mask_at, imps), 1) // GROUP,
        1.0, 0.0,
    ).astype(BF16)
    served = lax.broadcasted_iota(jnp.int32, (groups, advs), 1) // BLOCK * n_adv + me_a
    barred = jnp.full((groups, advs), -FAR, F32)
    counts = cnt_ref[...]
    for k in range(slots):
        named = jnp.where(counts > k, blk_ref[:, k : k + 1], -1)
        barred = jnp.where(named == served, 0.0, barred)
    aaug[mask_at : mask_at + groups, :] = barred.astype(BF16)
    if depth > mask_at + groups:
        aaug[mask_at + groups : depth, :] = jnp.zeros((depth - mask_at - groups, advs), BF16)

    row = lax.broadcasted_iota(jnp.int32, (ROWS, 128), 0)

    def put(ref, values, count, sign, first, ones):
        fixed = jnp.where((row >= ones) & (row < ones + 3), sign, 0.0)
        a, b, c = pieces(values * sign)
        for i in range(count):
            tile = jnp.where(row == first, a[i : i + 1, :], fixed)
            tile = jnp.where(row == first + 1, b[i : i + 1, :], tile)
            tile = jnp.where(row == first + 2, c[i : i + 1, :], tile)
            ref[head : head + ROWS, i * 128 : (i + 1) * 128] = tile.astype(BF16)

    pr[...] = jnp.zeros_like(pr)
    du[...] = jnp.zeros_like(du)
    put(vaug, du[...], groups, 1.0, 0, 3)

    def set_prices():
        put(aaug, pr[...], n_imp, -1.0, 3, 0)
        at[...] = aaug[...].T

    for s in range(1, n_imp):
        for copy in gather_copies(s):
            copy.wait_recv()
    for b in range(n_imp):
        aaug[0:feats, b * BLOCK : (b + 1) * BLOCK] = cat[b]
        lims[b : b + 1, :] = limb[b]
    set_prices()

    def tile_shares(rows, columns):
        scores = jnp.dot(at[rows, :], vaug[:, columns], preferred_element_type=F32)
        return jnp.minimum(jnp.maximum(scores, 0.0), 1.0)

    for it in range(ITERS):
        acc[...] = jnp.zeros_like(acc)

        def advance(c, carry):
            columns = pl.ds(pl.multiple_of(c * wide, wide), wide)
            demand = jnp.zeros((1, wide), F32)
            for t in range(advs // tall):
                rows = slice(t * tall, (t + 1) * tall)
                shares = tile_shares(rows, columns)
                demand = demand + jnp.sum(shares, axis=0, keepdims=True)
                total = shares[:, 0:GROUP]
                for h in range(1, wide // GROUP):
                    total = total + shares[:, h * GROUP : (h + 1) * GROUP]
                acc[rows, :] += total
            for h in range(wide // GROUP):
                demb[it, me_a, pl.ds(c * (wide // GROUP) + h, 1), :] = demand[:, h * GROUP : (h + 1) * GROUP]
            return carry

        lax.fori_loop(0, imps // wide, advance, 0)

        def demand_copy(s):
            slot = demb.at[it, me_a]
            return send(slot, slot, d_send.at[it, s], d_recv.at[it, s], {"adv": peer_a(s)})

        def outlay_copy(s):
            slot = outb.at[it, me_i]
            return send(slot, slot, o_send.at[it, s], o_recv.at[it, s], {"imp": peer_i(s)})

        for s in range(1, n_adv):
            demand_copy(s).start()
        for b in range(n_imp):
            outb[it, me_i, b : b + 1, :] = jnp.sum(
                acc[b * BLOCK : (b + 1) * BLOCK, :].T, axis=0, keepdims=True
            )
        for s in range(1, n_imp):
            outlay_copy(s).start()
        for s in range(1, n_adv):
            demand_copy(s).wait_recv()
        demand = demb[it, 0]
        for a in range(1, n_adv):
            demand = demand + demb[it, a]
        du[...] = jnp.maximum(du[...] + demand / cap_ref[...] - 1.0, 0.0)
        put(vaug, du[...], groups, 1.0, 0, 3)
        for s in range(1, n_imp):
            outlay_copy(s).wait_recv()
        outlay = outb[it, 0]
        for b in range(1, n_imp):
            outlay = outlay + outb[it, b]
        pr[...] = jnp.maximum(pr[...] + outlay / lims[...] - 1.0, 0.0)
        set_prices()

    def imp_terms(s, c):
        base = peer_a(s) * share + c * wide
        columns = pl.ds(pl.multiple_of(base, wide), wide)
        total = jnp.zeros((feats, wide), F32)
        for t in range(advs // tall):
            rows = slice(t * tall, (t + 1) * tall)
            weights = tile_shares(rows, columns).astype(BF16)
            w[rows, columns] = weights
            total = total + jnp.dot(aaug[0:feats, rows], weights, preferred_element_type=F32)
        return total

    def imp_copy(s):
        return send(igs.at[s], igr.at[s], i_send.at[s], i_recv.at[s], {"adv": peer_a(s)})

    def imp_step(s, carry):
        for c in range(share // wide):
            igs[s, :, c * wide : (c + 1) * wide] = imp_terms(s, c).astype(BF16)
        imp_copy(s).start()
        return carry

    lax.fori_loop(1, n_adv, imp_step, 0)
    for c in range(share // wide):
        igown[:, c * wide : (c + 1) * wide] = imp_terms(0, c)

    def adv_terms(s):
        rows = pl.ds(pl.multiple_of(peer_i(s) * BLOCK, BLOCK), BLOCK)
        terms = lax.dot_general(
            vaug[0:feats, :], w[rows, :], (((1,), (1,)), ((), ())), preferred_element_type=F32
        )
        return (terms * (1.0 / GROUP)).astype(BF16)

    def adv_copy(s):
        return send(ags.at[s], agr.at[s], a_send.at[s], a_recv.at[s], {"imp": peer_i(s)})

    def adv_step(s, carry):
        ags[s] = adv_terms(s)
        adv_copy(s).start()
        return carry

    lax.fori_loop(1, n_imp, adv_step, 0)
    own = adv_terms(0).astype(F32)
    prices_ref[...] = pr[pl.ds(me_i, 1), :]
    duals_ref[...] = du[...]
    for s in range(1, n_adv):
        imp_copy(s).wait_recv()
    total = igown[...]
    for s in range(1, n_adv):
        total = total + igr[s].astype(F32)
    ig_ref[...] = total.astype(BF16)
    for s in range(1, n_imp):
        adv_copy(s).wait_recv()
        own = own + agr[s].astype(F32)
    ag_ref[...] = own.astype(BF16)

    for s in range(1, n_imp):
        for copy in gather_copies(s):
            copy.wait_send()
        for it in range(ITERS):
            slot = outb.at[it, me_i]
            send(slot, slot, o_send.at[it, s], o_recv.at[it, s], {"imp": peer_i(s)}).wait_send()
        adv_copy(s).wait_send()
    for s in range(1, n_adv):
        for it in range(ITERS):
            slot = demb.at[it, me_a]
            send(slot, slot, d_send.at[it, s], d_recv.at[it, s], {"adv": peer_a(s)}).wait_send()
        imp_copy(s).wait_send()


def local(impression_vectors, advertiser_vectors, spend_limits, capacity, blocks, counts):
    feats, imps = impression_vectors.shape
    groups, _, slots = blocks.shape
    n_imp, n_adv = lax.axis_size("imp"), lax.axis_size("adv")
    advs = n_imp * BLOCK
    depth = -(-(feats + ROWS + groups) // 128) * 128
    share = imps // n_adv
    wide = min(256, share)
    tall = min(1024, advs)
    dma = pltpu.SemaphoreType.DMA
    vmem = pl.BlockSpec(memory_space=pltpu.VMEM)
    prices, duals, imp_grad, adv_grad = pl.pallas_call(
        functools.partial(kernel, n_imp, n_adv, (feats, groups, slots, depth, wide, tall)),
        out_shape=(
            jax.ShapeDtypeStruct((1, BLOCK), F32),
            jax.ShapeDtypeStruct((groups, GROUP), F32),
            jax.ShapeDtypeStruct((feats, share), BF16),
            jax.ShapeDtypeStruct((feats, BLOCK), BF16),
        ),
        in_specs=[vmem] * 6,
        out_specs=(vmem,) * 4,
        scratch_shapes=[
            pltpu.VMEM((depth, imps), BF16),
            pltpu.VMEM((depth, advs), BF16),
            pltpu.VMEM((advs, depth), BF16),
            pltpu.VMEM((n_imp, feats, BLOCK), BF16),
            pltpu.VMEM((n_imp, 1, BLOCK), F32),
            pltpu.VMEM((n_imp, BLOCK), F32),
            pltpu.VMEM((advs, GROUP), F32),
            pltpu.VMEM((ITERS, n_imp, n_imp, BLOCK), F32),
            pltpu.VMEM((ITERS, n_adv, groups, GROUP), F32),
            pltpu.VMEM((n_imp, BLOCK), F32),
            pltpu.VMEM((groups, GROUP), F32),
            pltpu.VMEM((advs, imps), BF16),
            pltpu.VMEM((n_adv, feats, share), BF16),
            pltpu.VMEM((n_adv, feats, share), BF16),
            pltpu.VMEM((feats, share), F32),
            pltpu.VMEM((n_imp, feats, BLOCK), BF16),
            pltpu.VMEM((n_imp, feats, BLOCK), BF16),
            dma((n_imp,)), dma((n_imp,)), dma((n_imp,)), dma((n_imp,)),
            dma((ITERS, n_imp)), dma((ITERS, n_imp)), dma((ITERS, n_adv)), dma((ITERS, n_adv)),
            dma((n_adv,)), dma((n_adv,)), dma((n_imp,)), dma((n_imp,)),
        ],
        compiler_params=pltpu.CompilerParams(
            collective_id=0, has_side_effects=True, vmem_limit_bytes=48 * 1024 * 1024
        ),
    )(
        impression_vectors,
        advertiser_vectors,
        spend_limits.reshape(1, BLOCK),
        capacity.reshape(groups, GROUP),
        blocks.reshape(groups, slots),
        counts,
    )
    return prices.reshape(-1), duals.reshape(-1), imp_grad, adv_grad


def solution(mesh):
    return jax.shard_map(
        local,
        mesh=mesh,
        in_specs=(
            P(None, "imp"),
            P(None, ("imp", "adv")),
            P(("imp", "adv")),
            P("imp"),
            P("imp", "adv", None),
            P("imp", "adv"),
        ),
        out_specs=(P(("imp", "adv")), P("imp"), P(None, ("imp", "adv")), P(None, ("imp", "adv"))),
        check_vma=False,
    )
```
